32 devices in a mesh: groups: 2 (over y), dp: 4 (over z), mp: 2 (over x), sub: 2 (over core).
Axes of the slice: x: 2, y: 2, z: 4, core: 2. Of those that a mesh axis runs over, the one named last changes fastest.
Arguments:
- tokens: bfloat16 [4096, 8192], P(('groups', 'dp'), ('mp', 'sub')), parts along dimension 0, may hold values from -6 to 6
- base_weight: bfloat16 [8192, 1024], P(('mp', 'sub')), may hold values from -0.0625 to 0.0625
- tenant_down_matrix: bfloat16 [64, 8192, 64], P(('groups', 'dp'), ('mp', 'sub')), parts along dimension 0, may hold values from -0.0625 to 0.0625
- tenant_up_matrix: bfloat16 [64, 64, 1024], P(('groups', 'dp'), None, ('mp', 'sub')), parts along dimension 0, may hold values from -0.75 to 0.75
- cotangent: bfloat16 [4096, 1024], P(('groups', 'dp'), ('mp', 'sub')), parts along dimension 0, may hold values from -6 to 6
- tenant: int32 [4096, 1], P(('groups', 'dp')), parts along dimension 0, may hold values from 0 to 31; in each aligned block of 512 rows (0 to 511, 512 to 1023, ...) at most 32 rows name the same one
Outputs:
- adapted_layer_output: bfloat16 [4096, 1024], P(('groups', 'dp'), ('mp', 'sub')), parts along dimension 0
- token_grad: bfloat16 [4096, 8192], P(('groups', 'dp'), ('mp', 'sub')), parts along dimension 0
- down_gradient: float32 [64, 8192, 64], P(('groups', 'dp'), ('mp', 'sub')), parts along dimension 0
- up_gradient: float32 [64, 64, 1024], P(('groups', 'dp'), None, ('mp', 'sub')), parts along dimension 0
The draws below stay inside these ranges and needn't reach their ends.
There are 2 independent parts, one for each index of `groups`. The reference program is written for one: setup_inputs(seed, part) draws one part's arguments, and reference() takes and returns one part's arrays. A program takes and returns all parts, laid end to end along the dimension named above; an argument that names none is the same for every part. Nothing has to cross between parts.
Inputs may be any that keep to these rules, and one draw needn't show every extreme that they name: The tokens of each index of dp name each tenant at most 32 times, and for every index of dp some tenant is named exactly 32 times.
All inputs are finite; a program needn't handle non-finite values.
Results may differ from the reference program's by a relative error of at most 0.004.
Values may be sent and summed in bfloat16 or wider, within the bound.
A program may use at most 128 MiB of HBM per device.

```python
import math
import jax
import jax.numpy as jnp
import numpy as np
from jax import lax

MODEL_WIDTH = 8192
KEY_WIDTH = 1024
R = 64
TENANTS = 32
TOK_DEV = 512
CAP = 32
TOKEN_TOTAL = 2048
N_DP = 4


def levels(rng, extent, split, least, top_value):
    def one(position, blocks):
        heights = jax.random.uniform(jax.random.fold_in(jax.random.fold_in(rng, 6), position), (blocks,), jnp.float32, least / len(split), top_value / len(split))
        return jnp.repeat(jnp.exp(heights), extent[position] // blocks).reshape((-1,) + (1,) * (len(extent) - position - 1))

    gain = one(*split[0])
    for cut in split[1:]:
        gain = gain * one(*cut)
    return gain


def shared_out(rng, own, number, rows, count, top, bound, lean):
    sequence = jax.random.permutation(rng, count)
    heavy_load, ordinary = portions_of(count, rows * top, bound, lean, True), portions_of(count, rows * top, bound, lean, False)
    places = jnp.arange(count)

    def named(tallies, turn):
        used = int((tallies > 0).sum())
        fixed = max(1, used // 4)
        passed = fixed + (places - fixed + turn * (used - fixed)) % max(1, count - fixed)
        return jnp.zeros((count,), jnp.int32).at[sequence[jnp.where(places < fixed, places, passed)]].set(jnp.asarray(tallies, jnp.int32))

    tallies = jnp.where(number % 4 == 0, named(heavy_load, number // 4), named(ordinary, number - number // 4 - 1))
    mixed = jax.random.permutation(jax.random.fold_in(own, 3), count)
    source_of, sink = mixed[0:count // 2 * 2:2], mixed[1:count // 2 * 2:2]
    slack = jnp.minimum(tallies[source_of] - 1, bound - tallies[sink]) // 2
    slack = jnp.where((source_of == sequence[0]) | (sink == sequence[0]) | (tallies[sink] == 0), 0, jnp.maximum(slack, 0))
    passed = jax.random.randint(jax.random.fold_in(own, 4), (count // 2,), 0, 1 << 20) % (slack + 1)
    tallies = tallies.at[source_of].add(-passed).at[sink].add(passed)
    members = jnp.searchsorted(jnp.cumsum(tallies), jnp.arange(rows * top), side="right").astype(jnp.int32)
    table = members.reshape(top, rows).T
    table = table[jax.random.permutation(jax.random.fold_in(own, 1), rows)]
    turn = jax.random.randint(jax.random.fold_in(own, 2), (rows, 1), 0, top)
    return jnp.take_along_axis(table, (jnp.arange(top)[None, :] + turn) % top, axis=1)


def portions_of(number_of, total, bound, skew, full):
    weights = [(1 << 20) // math.isqrt(standing ** skew) + 1 for standing in range(1, number_of + 1)]
    largest = bound if full else min(bound, max(-(-total // number_of), total * weights[0] // sum(weights)))
    least = 1 if total - largest >= number_of - 1 else 0
    given, rest = [largest] + [least] * (number_of - 1), total - largest - least * (number_of - 1)
    while rest > 0:
        free = [i for i in range(1, number_of) if given[i] < largest] or [i for i in range(1, number_of) if given[i] < bound]
        pool, remaining = sum([weights[i] for i in free]), rest
        for i in free:
            more = min(bound - given[i], max(1, remaining * weights[i] // pool), rest)
            given[i] = given[i] + more
            rest = rest - more
    return np.array(given)


def gaussian(rng, extent, deviation, most, split=(), kind=jnp.bfloat16):
    array = deviation * jax.random.normal(rng, extent, jnp.float32)
    if split:
        array = array * levels(rng, extent, split, -0.22, 0.18)
    return jnp.clip(array, -most, most).astype(kind)


def setup_inputs(seed: int = 0, part: int = 0) -> dict:
    key_of = jax.random.split(jax.random.key(seed), 7)
    part_splits = jax.random.split(jax.random.fold_in(key_of[6], part), 7)
    tokens = gaussian(part_splits[0], (TOKEN_TOTAL, MODEL_WIDTH), 1.0, 6.0, ((0, 4), (1, 4)))
    base_weight = gaussian(key_of[1], (MODEL_WIDTH, KEY_WIDTH), MODEL_WIDTH ** -0.5, 0.0625, ((0, 4),))
    tenant_down_matrix = gaussian(part_splits[2], (TENANTS, MODEL_WIDTH, R), MODEL_WIDTH ** -0.5, 0.0625, ((0, 4), (1, 4)))
    tenant_up_matrix = gaussian(part_splits[3], (TENANTS, R, KEY_WIDTH), R ** -0.5, 0.75, ((0, 4), (2, 4)))
    cotangent = gaussian(part_splits[4], (TOKEN_TOTAL, KEY_WIDTH), 1.0, 6.0, ((0, 4), (1, 4)))
    tenant_keys = jax.random.split(jax.random.fold_in(part_splits[5], 1), TOKEN_TOTAL // TOK_DEV)
    tenant_turns = jax.random.permutation(jax.random.fold_in(part_splits[5], 3), TOKEN_TOTAL // TOK_DEV)
    tenant = jax.vmap(lambda own, number: shared_out(jax.random.fold_in(part_splits[5], 2), own, number, TOK_DEV, TENANTS, 1, CAP, 2))(tenant_keys, tenant_turns).reshape((TOKEN_TOTAL, 1))
    return {"tokens": tokens, "base_weight": base_weight, "tenant_down_matrix": tenant_down_matrix, "tenant_up_matrix": tenant_up_matrix, "cotangent": cotangent, "tenant": tenant}


adapter_scale = 0.5


def reference(tokens, base_weight, tenant_down_matrix, tenant_up_matrix, cotangent, tenant):
    exact_precision = lax.Precision.HIGHEST
    tenant_ids = tenant[:, 0].reshape(N_DP, TOK_DEV)
    onehot = (tenant_ids[:, :, None] == jnp.arange(TENANTS, dtype=jnp.int32)[None, None, :]).astype(jnp.int32)
    in_tenant = jnp.sum(onehot * (jnp.cumsum(onehot, axis=1) - 1), axis=2)
    devices = jnp.arange(N_DP, dtype=jnp.int32)[:, None]
    flat_index = (tenant_ids * (N_DP * CAP) + devices * CAP + in_tenant).reshape(-1).astype(jnp.int32)
    row_lookup = jnp.full((TENANTS * N_DP * CAP,), TOKEN_TOTAL, jnp.int32)
    row_lookup = row_lookup.at[flat_index].set(jnp.arange(TOKEN_TOTAL, dtype=jnp.int32)).reshape(TENANTS, N_DP * CAP)
    padded_x = jnp.concatenate([tokens, jnp.zeros((1, MODEL_WIDTH), jnp.bfloat16)], axis=0)
    padded_g = jnp.concatenate([cotangent, jnp.zeros((1, KEY_WIDTH), jnp.bfloat16)], axis=0)

    def tenant_split(args):
        row_index, down_tile, up_tile = args
        input_rows = padded_x[row_index].astype(jnp.float32)
        gradient_rows = padded_g[row_index].astype(jnp.float32)
        down_float = down_tile.astype(jnp.float32)
        up_float = up_tile.astype(jnp.float32)
        rank_output = lax.optimization_barrier(jnp.dot(input_rows, down_float, precision=exact_precision).astype(jnp.bfloat16)).astype(jnp.float32)
        rank_backward = lax.optimization_barrier(jnp.dot(gradient_rows, up_float.T, precision=exact_precision).astype(jnp.bfloat16)).astype(jnp.float32)
        adapter_output = (adapter_scale * jnp.dot(rank_output, up_float, precision=exact_precision)).astype(jnp.bfloat16)
        adapter_input_gradient = (adapter_scale * jnp.dot(rank_backward, down_float.T, precision=exact_precision)).astype(jnp.bfloat16)
        down_gradient = adapter_scale * jnp.dot(input_rows.T, rank_backward, precision=exact_precision)
        up_gradient = adapter_scale * jnp.dot(rank_output.T, gradient_rows, precision=exact_precision)
        return adapter_output, adapter_input_gradient, down_gradient, up_gradient

    adapter_output, adapter_input_gradient, down_gradient, up_gradient = lax.map(tenant_split, (row_lookup, tenant_down_matrix, tenant_up_matrix))
    flattened_rows = row_lookup.reshape(-1)
    adapter_token = jnp.zeros((TOKEN_TOTAL + 1, KEY_WIDTH), jnp.bfloat16).at[flattened_rows].set(adapter_output.reshape(-1, KEY_WIDTH))[:TOKEN_TOTAL]
    token_input_gradient = jnp.zeros((TOKEN_TOTAL + 1, MODEL_WIDTH), jnp.bfloat16).at[flattened_rows].set(adapter_input_gradient.reshape(-1, MODEL_WIDTH))[:TOKEN_TOTAL]
    frozen_output = jnp.dot(tokens.astype(jnp.float32), base_weight.astype(jnp.float32), precision=exact_precision)
    adapted_layer_output = (frozen_output + adapter_token.astype(jnp.float32)).astype(jnp.bfloat16)
    dx_base = jnp.dot(cotangent.astype(jnp.float32), base_weight.astype(jnp.float32).T, precision=exact_precision)
    token_grad = (dx_base + token_input_gradient.astype(jnp.float32)).astype(jnp.bfloat16)
    return adapted_layer_output, token_grad, down_gradient, up_gradient
```

```python
import jax
import jax.numpy as jnp
from jax import lax
from jax.sharding import PartitionSpec as P

adapter_scale = 0.5
f32 = jnp.float32
bf16 = jnp.bfloat16


def dot(a, b, ca, cb):
    return lax.dot_general(a, b, (((ca,), (cb,)), ((), ())), preferred_element_type=f32)


def local(tokens, base_weight, down, up, cotangent, tenant):
    groups = lax.axis_size("dp")
    own, width, rank = down.shape
    rows = tokens.shape[0]
    key_width = cotangent.shape[1]
    total = groups * own
    slots = own * (2 * rows // total)
    ids = tenant[:, 0]
    me = lax.axis_index("dp")
    down_rows = jnp.transpose(down, (0, 2, 1)).reshape(own * rank, width)
    up_rows = up.reshape(own * rank, key_width)

    holder = ids // own
    holds = (holder[:, None] == jnp.arange(groups, dtype=jnp.int32)[None, :]).astype(jnp.int32)
    place = jnp.sum(holds * (jnp.cumsum(holds, axis=0) - 1), axis=1)

    def shifted(array, step):
        if step == 0:
            return array
        return lax.ppermute(array, "dp", [(i, (i + step) % groups) for i in range(groups)])

    slot = jnp.arange(slots, dtype=jnp.int32)
    picks, x_in, g_in, own_in = [], [], [], []
    for step in range(groups):
        to = lax.rem(me + step, groups)
        pick = (holder[None, :] == to) & (place[None, :] == slot[:, None])
        tenant_of = jnp.max(jnp.where(pick, ids[None, :] - to * own, -1), axis=1)
        pick = pick.astype(bf16)
        picks.append(pick)
        own_in.append(shifted(tenant_of, step))
        g_in.append(shifted(dot(pick, cotangent, 1, 0).astype(bf16), step))
        x_in.append(shifted(dot(pick, tokens, 1, 0).astype(bf16), step))

    owner = jnp.arange(own * rank, dtype=jnp.int32) // rank
    masks = [t[:, None] == owner[None, :] for t in own_in]
    mask = jnp.concatenate(masks, 0)

    def fold(wide):
        return jnp.where(mask, wide, 0.0).reshape(-1, own, rank).sum(1)

    def spread(narrow):
        return jnp.where(mask, jnp.tile(narrow, (1, own)), jnp.zeros((), bf16))

    g_here = jnp.concatenate(g_in, 0)
    back = lax.psum(fold(dot(g_here, up_rows, 1, 1)), ("mp", "sub")).astype(bf16)
    back = spread(back)
    lora_dx = jnp.zeros((rows, width), f32)
    for step in range(groups):
        part = back[step * slots : (step + 1) * slots]
        term = (adapter_scale * dot(part, down_rows, 1, 0)).astype(bf16)
        term = shifted(term, (groups - step) % groups)
        lora_dx = lora_dx + dot(picks[step], term, 0, 0)

    x_here = jnp.concatenate(x_in, 0)
    out_rank = lax.psum(fold(dot(x_here, down_rows, 1, 1)), ("mp", "sub")).astype(bf16)
    out_rank = spread(out_rank)
    lora_out = jnp.zeros((rows, key_width), f32)
    for step in range(groups):
        part = out_rank[step * slots : (step + 1) * slots]
        term = (adapter_scale * dot(part, up_rows, 1, 0)).astype(bf16)
        term = shifted(term, (groups - step) % groups)
        lora_out = lora_out + dot(picks[step], term, 0, 0)

    down_grad = adapter_scale * dot(back, x_here, 0, 0)
    down_grad = jnp.transpose(down_grad.reshape(own, rank, width), (0, 2, 1))
    up_grad = (adapter_scale * dot(out_rank, g_here, 0, 0)).reshape(own, rank, key_width)

    frozen = lax.psum_scatter(
        dot(tokens, base_weight, 1, 0), ("mp", "sub"), scatter_dimension=1, tiled=True
    )
    g_wide = lax.all_gather(cotangent, ("mp", "sub"), axis=1, tiled=True)
    out = (frozen + lora_out).astype(bf16)
    token_grad = (dot(g_wide, base_weight, 1, 1) + lora_dx).astype(bf16)
    return out, token_grad, down_grad, up_grad


def solution(mesh):
    rows = P(("groups", "dp"), ("mp", "sub"))
    downs = P(("groups", "dp"), ("mp", "sub"), None)
    ups = P(("groups", "dp"), None, ("mp", "sub"))
    return jax.shard_map(
        local,
        mesh=mesh,
        in_specs=(rows, P(("mp", "sub"), None), downs, ups, rows, P(("groups", "dp"), None)),
        out_specs=(rows, rows, downs, ups),
        check_vma=False,
    )
```

```python
import jax
import jax.numpy as jnp
from jax import lax
from jax.sharding import PartitionSpec as P

adapter_scale = 0.5
f32 = jnp.float32
bf16 = jnp.bfloat16


def dot(a, b, ca, cb):
    return lax.dot_general(a, b, (((ca,), (cb,)), ((), ())), preferred_element_type=f32)


def body(tokens, base_weight, down, up, cotangent, ids, holder, place, slots):
    groups = lax.axis_size("dp")
    own, width, rank = down.shape
    rows = tokens.shape[0]
    key_width = cotangent.shape[1]
    me = lax.axis_index("dp")
    down_rows = jnp.transpose(down, (0, 2, 1)).reshape(own * rank, width)
    up_rows = up.reshape(own * rank, key_width)

    def shifted(array, step):
        if step == 0:
            return array
        return lax.ppermute(array, "dp", [(i, (i + step) % groups) for i in range(groups)])

    slot = jnp.arange(slots, dtype=jnp.int32)
    steps = [(2 * groups - 1 - k) % groups for k in range(groups)]
    picks, x_in, g_in, own_in = {}, {}, {}, {}
    for step in steps:
        to = lax.rem(me + step, groups)
        pick = (holder[None, :] == to) & (place[None, :] == slot[:, None])
        tenant_of = jnp.max(jnp.where(pick, ids[None, :] - to * own, -1), axis=1)
        picks[step] = pick.astype(bf16)
        own_in[step] = shifted(tenant_of, step)
        g_in[step] = dot(picks[step], cotangent, 1, 0).astype(bf16)
    packed, tokens_later = lax.optimization_barrier((g_in, tokens))
    for step in steps:
        g_in[step] = shifted(packed[step], step)
        x_in[step] = shifted(dot(picks[step], tokens_later, 1, 0).astype(bf16), step)

    owner = jnp.arange(own * rank, dtype=jnp.int32) // rank
    mask = jnp.concatenate([own_in[s] for s in steps], 0)[:, None] == owner[None, :]

    def fold(wide):
        return jnp.where(mask, wide, 0.0).reshape(-1, own, rank).sum(1)

    def spread(narrow):
        return jnp.where(mask, jnp.tile(narrow, (1, own)), jnp.zeros((), bf16))

    g_here = jnp.concatenate([g_in[s] for s in steps], 0)
    back = lax.psum(fold(dot(g_here, up_rows, 1, 1)), ("mp", "sub")).astype(bf16)
    back = spread(back)
    terms = []
    for k, step in enumerate(steps):
        part = back[k * slots : (k + 1) * slots]
        term = (adapter_scale * dot(part, down_rows, 1, 0)).astype(bf16)
        terms.append(term)
    terms = [shifted(t, (groups - s) % groups) for t, s in zip(terms, steps)]

    x_here = jnp.concatenate([x_in[s] for s in steps], 0)
    x_here, back = lax.optimization_barrier((x_here, back))
    out_rank = lax.psum(fold(dot(x_here, down_rows, 1, 1)), ("mp", "sub")).astype(bf16)
    out_rank = spread(out_rank)
    lora_out = jnp.zeros((rows, key_width), f32)
    for k, step in enumerate(steps):
        part = out_rank[k * slots : (k + 1) * slots]
        term = (adapter_scale * dot(part, up_rows, 1, 0)).astype(bf16)
        term = shifted(term, (groups - step) % groups)
        lora_out = lora_out + dot(picks[step], term, 0, 0)

    down_grad = adapter_scale * dot(back, x_here, 0, 0)
    down_grad = jnp.transpose(down_grad.reshape(own, rank, width), (0, 2, 1))
    up_grad = (adapter_scale * dot(out_rank, g_here, 0, 0)).reshape(own, rank, key_width)

    frozen = lax.psum_scatter(
        dot(tokens, base_weight, 1, 0), ("mp", "sub"), scatter_dimension=1, tiled=True
    )
    g_wide = lax.all_gather(cotangent, ("mp", "sub"), axis=1, tiled=True)
    out = (frozen + lora_out).astype(bf16)
    dx = dot(g_wide, base_weight, 1, 1)
    for step, term in zip(steps, terms):
        dx = dx + dot(picks[step], term, 0, 0)
    return out, dx.astype(bf16), down_grad, up_grad


def local(tokens, base_weight, down, up, cotangent, tenant):
    groups = lax.axis_size("dp")
    own = down.shape[0]
    most = own * (2 * tokens.shape[0] // (groups * own))
    usual = -(-(most * 3 // 4) // 16) * 16
    ids = tenant[:, 0]
    holder = ids // own
    holds = (holder[:, None] == jnp.arange(groups, dtype=jnp.int32)[None, :]).astype(jnp.int32)
    place = jnp.sum(holds * (jnp.cumsum(holds, axis=0) - 1), axis=1)
    args = (tokens, base_weight, down, up, cotangent, ids, holder, place)
    if usual >= most:
        return body(*args, most)
    results = body(*args, usual)
    fullest = lax.pmax(jnp.max(place), ("groups", "dp"))
    return lax.cond(fullest >= usual, lambda r: body(*args, most), lambda r: r, results)


def solution(mesh):
    rows = P(("groups", "dp"), ("mp", "sub"))
    downs = P(("groups", "dp"), ("mp", "sub"), None)
    ups = P(("groups", "dp"), None, ("mp", "sub"))
    return jax.shard_map(
        local,
        mesh=mesh,
        in_specs=(rows, P(("mp", "sub"), None), downs, ups, rows, P(("groups", "dp"), None)),
        out_specs=(rows, rows, downs, ups),
        check_vma=False,
    )
```

```python
import functools

import jax
import jax.numpy as jnp
from jax import lax
from jax.sharding import PartitionSpec as P

adapter_scale = 0.5
f32 = jnp.float32
bf16 = jnp.bfloat16


def dot(a, b, ca, cb):
    return lax.dot_general(a, b, (((ca,), (cb,)), ((), ())), preferred_element_type=f32)


def body(slots, tokens, base_weight, down, up, cotangent, g_wide, ids_all, place_all):
    groups = lax.axis_size("dp")
    own, width, rank = down.shape
    key_width = cotangent.shape[1]
    me = lax.axis_index("dp")
    down_rows = jnp.transpose(down, (0, 2, 1)).reshape(own * rank, width)
    up_rows = up.reshape(own * rank, key_width)

    def shifted(array, step):
        if step == 0:
            return array
        return lax.ppermute(array, "dp", [(i, (i + step) % groups) for i in range(groups)])

    slot = jnp.arange(slots, dtype=jnp.int32)

    def chosen(source, holder):
        ids = lax.dynamic_index_in_dim(ids_all, source, 0, keepdims=False)
        place = lax.dynamic_index_in_dim(place_all, source, 0, keepdims=False)
        hit = (ids // own == holder)[None, :] & (place[None, :] == slot[:, None])
        return ids, hit

    steps = list(range(1, groups)) + [0]
    picks, x_in, g_in, own_in = {}, {}, {}, {}
    for step in steps:
        picks[step] = chosen(me, lax.rem(me + step, groups))[1].astype(bf16)
        g_in[step] = dot(picks[step], cotangent, 1, 0).astype(bf16)
    packed, tokens_later = lax.optimization_barrier((g_in, tokens))
    for step in steps:
        g_in[step] = shifted(packed[step], step)
        x_in[step] = dot(picks[step], tokens_later, 1, 0).astype(bf16)
    for step in steps:
        x_in[step] = shifted(x_in[step], step)
        ids, hit = chosen(lax.rem(me + groups - step, groups), me)
        own_in[step] = jnp.max(jnp.where(hit, ids[None, :] - me * own, -1), axis=1)

    owner = jnp.arange(own * rank, dtype=jnp.int32) // rank
    mask = jnp.concatenate([own_in[s] for s in steps], 0)[:, None] == owner[None, :]

    def fold(wide):
        return jnp.where(mask, wide, 0.0).reshape(-1, own, rank).sum(1)

    def spread(narrow):
        return jnp.where(mask, jnp.tile(narrow, (1, own)), jnp.zeros((), bf16))

    g_here = jnp.concatenate([g_in[s] for s in steps], 0)
    back = lax.psum(fold(dot(g_here, up_rows, 1, 1)), ("mp", "sub")).astype(bf16)
    back = spread(back)
    dx_terms = []
    for k, step in enumerate(steps):
        part = back[k * slots : (k + 1) * slots]
        term = (adapter_scale * dot(part, down_rows, 1, 0)).astype(bf16)
        dx_terms.append(shifted(term, (groups - step) % groups))
    pick = jnp.concatenate([picks[s] for s in steps], 0)
    dx = dot(g_wide, base_weight, 1, 1)

    x_here = jnp.concatenate([x_in[s] for s in steps], 0)
    x_here, back, dx = lax.optimization_barrier((x_here, back, dx))
    out_rank = lax.psum(fold(dot(x_here, down_rows, 1, 1)), ("mp", "sub")).astype(bf16)
    out_rank = spread(out_rank)
    out_terms = []
    for k, step in enumerate(steps):
        part = out_rank[k * slots : (k + 1) * slots]
        term = (adapter_scale * dot(part, up_rows, 1, 0)).astype(bf16)
        out_terms.append(shifted(term, (groups - step) % groups))
    lora_out = dot(pick, jnp.concatenate(out_terms, 0), 0, 0)

    down_grad = adapter_scale * dot(back, x_here, 0, 0)
    down_grad = jnp.transpose(down_grad.reshape(own, rank, width), (0, 2, 1))
    up_grad = (adapter_scale * dot(out_rank, g_here, 0, 0)).reshape(own, rank, key_width)
    token_grad = (dx + dot(pick, jnp.concatenate(dx_terms, 0), 0, 0)).astype(bf16)
    return lora_out, token_grad, down_grad, up_grad


def local(tokens, base_weight, down, up, cotangent, tenant):
    groups = lax.axis_size("dp")
    own = down.shape[0]
    rows = tokens.shape[0]
    most = own * (2 * rows // (groups * own))
    copies = lax.axis_size("groups")
    at = lax.axis_index("groups") * groups + lax.axis_index("dp")
    table = jnp.zeros((copies * groups, rows), jnp.int32)
    table = lax.psum(
        lax.dynamic_update_slice(table, tenant.T, (at, jnp.int32(0))), ("groups", "dp")
    )
    holder = table // own
    holds = holder[:, :, None] == jnp.arange(groups, dtype=jnp.int32)[None, None, :]
    counts = jnp.cumsum(holds.astype(jnp.int32), axis=1)
    place = jnp.sum(jnp.where(holds, counts - 1, 0), axis=2)
    first = lax.axis_index("groups") * groups
    ids_all = lax.dynamic_slice_in_dim(table, first, groups, 0)
    place_all = lax.dynamic_slice_in_dim(place, first, groups, 0)

    frozen = lax.psum_scatter(
        dot(tokens, base_weight, 1, 0), ("mp", "sub"), scatter_dimension=1, tiled=True
    )
    g_wide = lax.all_gather(cotangent, ("mp", "sub"), axis=1, tiled=True)
    args = (tokens, base_weight, down, up, cotangent, g_wide, ids_all, place_all)
    sizes = sorted({min(most, -(-(most * part) // 256) * 16) for part in (9, 10, 11, 12, 13, 16)})
    if len(sizes) == 1:
        results = body(most, *args)
    else:
        fullest = jnp.max(place) + 1
        branch = sum((fullest > size).astype(jnp.int32) for size in sizes[:-1])
        results = lax.switch(branch, [functools.partial(body, size) for size in sizes], *args)
    lora_out, token_grad, down_grad, up_grad = results
    return (frozen + lora_out).astype(bf16), token_grad, down_grad, up_grad


def solution(mesh):
    rows = P(("groups", "dp"), ("mp", "sub"))
    downs = P(("groups", "dp"), ("mp", "sub"), None)
    ups = P(("groups", "dp"), None, ("mp", "sub"))
    return jax.shard_map(
        local,
        mesh=mesh,
        in_specs=(rows, P(("mp", "sub"), None), downs, ups, rows, P(("groups", "dp"), None)),
        out_specs=(rows, rows, downs, ups),
        check_vma=False,
    )
```

```python
import jax
import jax.numpy as jnp
from jax import lax
from jax.sharding import PartitionSpec as P

adapter_scale = 0.5
f32 = jnp.float32
bf16 = jnp.bfloat16


def dot(a, b, ca, cb):
    return lax.dot_general(a, b, (((ca,), (cb,)), ((), ())), preferred_element_type=f32)


def body(slots, tokens, base_weight, down, up, cotangent, ids, holder, place, fullest):
    groups = lax.axis_size("dp")
    own, width, rank = down.shape
    rows = tokens.shape[0]
    key_width = cotangent.shape[1]
    me = lax.axis_index("dp")
    down_rows = jnp.transpose(down, (0, 2, 1)).reshape(own * rank, width)
    up_rows = up.reshape(own * rank, key_width)
    code_rows = -(-own // 16) * 16

    def shifted(array, step):
        if step == 0:
            return array
        return lax.ppermute(array, "dp", [(i, (i + step) % groups) for i in range(groups)])

    def swapped(array):
        return lax.all_to_all(array, "dp", split_axis=0, concat_axis=0, tiled=True)

    seat = holder * slots + place
    seats = jnp.arange(groups * slots, dtype=jnp.int32)
    pick = ((seat[None, :] == seats[:, None]) & (place < slots)[None, :]).astype(bf16)
    local_id = jnp.arange(code_rows, dtype=jnp.int32)
    code = (lax.rem(ids, own)[:, None] == local_id[None, :]).astype(bf16)
    code = dot(code, pick, 0, 1).astype(bf16).reshape(code_rows, groups, slots)
    code = jnp.pad(jnp.transpose(code, (1, 0, 2)), ((0, 0), (0, 0), (0, key_width - slots)))
    packed = dot(pick, cotangent, 1, 0).astype(bf16).reshape(groups, slots, key_width)
    packed = jnp.concatenate([packed, code], 1)
    packed, tokens = lax.optimization_barrier((packed, tokens))
    got = swapped(packed)

    slot = jnp.arange(slots, dtype=jnp.int32)
    steps = list(range(1, groups)) + [0]
    x_out = []
    for step in steps:
        to = lax.rem(me + step, groups)
        hit = (holder[None, :] == to) & (place[None, :] == slot[:, None])
        x_out.append(dot(hit.astype(bf16), tokens, 1, 0).astype(bf16))
    x_out, tokens = lax.optimization_barrier((x_out, tokens))
    x_in = [shifted(x, step) for x, step in zip(x_out, steps)]
    sources = [lax.rem(me + groups - step, groups) for step in steps]
    frozen = lax.psum_scatter(
        dot(tokens, base_weight, 1, 0), ("mp", "sub"), scatter_dimension=1, tiled=True
    )

    got = [lax.dynamic_index_in_dim(got, source, 0, keepdims=False) for source in sources]
    g_here = jnp.concatenate([one[:slots] for one in got], 0)
    codes = jnp.concatenate([one[slots:, :slots] for one in got], 1)
    owner = jnp.arange(own * rank, dtype=jnp.int32) // rank
    mask = dot(codes, (local_id[:, None] == owner[None, :]).astype(bf16), 0, 0) > 0.5

    def fold(wide):
        return jnp.where(mask, wide, 0.0).reshape(-1, own, rank).sum(1)

    def spread(narrow):
        return jnp.where(mask, jnp.tile(narrow, (1, own)), jnp.zeros((), bf16))

    back = lax.psum(fold(dot(g_here, up_rows, 1, 1)), ("mp", "sub")).astype(bf16)
    back = spread(back)
    dx_terms = []
    for k, step in enumerate(steps):
        part = back[k * slots : (k + 1) * slots]
        dx_terms.append((adapter_scale * dot(part, down_rows, 1, 0)).astype(bf16))
    dx_terms, fullest = lax.optimization_barrier((dx_terms, fullest))
    dx_in = [shifted(t, (groups - s) % groups) for t, s in zip(dx_terms, steps)]
    fullest = lax.pmax(fullest, ("groups", "dp"))
    g_wide = lax.all_gather(cotangent, ("mp", "sub"), axis=1, tiled=True)
    dx = dot(g_wide, base_weight, 1, 1)

    x_here = jnp.concatenate(x_in, 0)
    x_here, back, dx, fullest = lax.optimization_barrier((x_here, back, dx, fullest))
    out_rank = lax.psum(fold(dot(x_here, down_rows, 1, 1)), ("mp", "sub")).astype(bf16)
    out_rank = spread(out_rank)
    out_term = (adapter_scale * dot(out_rank, up_rows, 1, 0)).astype(bf16)
    out_term = out_term.reshape(groups, slots, key_width)
    order = [lax.rem(me + 2 * groups - s - 1, groups) for s in range(groups)]
    out_term = jnp.stack(
        [lax.dynamic_index_in_dim(out_term, o, 0, keepdims=False) for o in order]
    )
    out_term = swapped(out_term).reshape(groups * slots, key_width)
    lora_out = dot(pick, out_term, 0, 0)

    down_grad = adapter_scale * dot(back, x_here, 0, 0)
    down_grad = jnp.transpose(down_grad.reshape(own, rank, width), (0, 2, 1))
    up_grad = (adapter_scale * dot(out_rank, g_here, 0, 0)).reshape(own, rank, key_width)
    for term, step in zip(dx_in, steps):
        to = lax.rem(me + step, groups)
        hit = (holder[None, :] == to) & (place[None, :] == slot[:, None])
        dx = dx + dot(hit.astype(bf16), term, 0, 0)
    out = (frozen + lora_out).astype(bf16)
    return (out, dx.astype(bf16), down_grad, up_grad), fullest


def local(tokens, base_weight, down, up, cotangent, tenant):
    groups = lax.axis_size("dp")
    own = down.shape[0]
    most = own * (2 * tokens.shape[0] // (groups * own))
    usual = min(most, -(-(most * 13) // 256) * 16)
    ids = tenant[:, 0]
    holder = ids // own
    holds = holder[:, None] == jnp.arange(groups, dtype=jnp.int32)[None, :]
    counts = jnp.cumsum(holds.astype(jnp.int32), axis=0)
    place = jnp.sum(jnp.where(holds, counts - 1, 0), axis=1)
    args = (tokens, base_weight, down, up, cotangent, ids, holder, place, jnp.max(place))
    results, fullest = body(usual, *args)
    if usual == most:
        return results
    return lax.cond(fullest >= usual, lambda r: body(most, *args)[0], lambda r: r, results)


def solution(mesh):
    rows = P(("groups", "dp"), ("mp", "sub"))
    downs = P(("groups", "dp"), ("mp", "sub"), None)
    ups = P(("groups", "dp"), None, ("mp", "sub"))
    return jax.shard_map(
        local,
        mesh=mesh,
        in_specs=(rows, P(("mp", "sub"), None), downs, ups, rows, P(("groups", "dp"), None)),
        out_specs=(rows, rows, downs, ups),
        check_vma=False,
    )
```

```python
import jax
import jax.numpy as jnp
from jax import lax
from jax.sharding import PartitionSpec as P

adapter_scale = 0.5
f32 = jnp.float32
bf16 = jnp.bfloat16


def dot(a, b, ca, cb):
    return lax.dot_general(a, b, (((ca,), (cb,)), ((), ())), preferred_element_type=f32)


def body(slots, tokens, base_weight, down, up, cotangent, ids, holder, place, fullest):
    groups = lax.axis_size("dp")
    own, width, rank = down.shape
    rows = tokens.shape[0]
    key_width = cotangent.shape[1]
    me = lax.axis_index("dp")
    down_rows = jnp.transpose(down, (0, 2, 1)).reshape(own * rank, width)
    up_rows = up.reshape(own * rank, key_width)
    code_rows = -(-own // 16) * 16
    g_wide = lax.all_gather(cotangent, ("mp", "sub"), axis=1, tiled=True)

    def shifted(array, step):
        if step == 0:
            return array
        return lax.ppermute(array, "dp", [(i, (i + step) % groups) for i in range(groups)])

    def swapped(array):
        return lax.all_to_all(array, "dp", split_axis=0, concat_axis=0, tiled=True)

    seat = holder * slots + place
    seats = jnp.arange(groups * slots, dtype=jnp.int32)
    pick = ((seat[None, :] == seats[:, None]) & (place < slots)[None, :]).astype(bf16)
    local_id = jnp.arange(code_rows, dtype=jnp.int32)
    code = (lax.rem(ids, own)[:, None] == local_id[None, :]).astype(bf16)
    code = dot(code, pick, 0, 1).astype(bf16).reshape(code_rows, groups, slots)
    code = jnp.pad(jnp.transpose(code, (1, 0, 2)), ((0, 0), (0, 0), (0, key_width - slots)))
    packed = dot(pick, cotangent, 1, 0).astype(bf16).reshape(groups, slots, key_width)
    packed = jnp.concatenate([packed, code], 1)
    packed, tokens = lax.optimization_barrier((packed, tokens))
    got = swapped(packed)

    slot = jnp.arange(slots, dtype=jnp.int32)
    steps = list(range(1, groups)) + [0]
    x_out = []
    for step in steps:
        to = lax.rem(me + step, groups)
        hit = (holder[None, :] == to) & (place[None, :] == slot[:, None])
        x_out.append(dot(hit.astype(bf16), tokens, 1, 0).astype(bf16))
    x_out, got, tokens = lax.optimization_barrier((x_out, got, tokens))
    x_in = [shifted(x, step) for x, step in zip(x_out, steps)]
    sources = [lax.rem(me + groups - step, groups) for step in steps]

    got = [lax.dynamic_index_in_dim(got, source, 0, keepdims=False) for source in sources]
    g_here = jnp.concatenate([one[:slots] for one in got], 0)
    codes = jnp.concatenate([one[slots:, :slots] for one in got], 1)
    owner = jnp.arange(own * rank, dtype=jnp.int32) // rank
    mask = dot(codes, (local_id[:, None] == owner[None, :]).astype(bf16), 0, 0) > 0.5

    def fold(wide):
        return jnp.where(mask, wide, 0.0).reshape(-1, own, rank).sum(1)

    def spread(narrow):
        return jnp.where(mask, jnp.tile(narrow, (1, own)), jnp.zeros((), bf16))

    back = lax.psum(fold(dot(g_here, up_rows, 1, 1)), ("mp", "sub")).astype(bf16)
    back = spread(back)
    dx_terms = []
    for k, step in enumerate(steps):
        part = back[k * slots : (k + 1) * slots]
        dx_terms.append((adapter_scale * dot(part, down_rows, 1, 0)).astype(bf16))
    dx_terms, tokens, g_wide = lax.optimization_barrier((dx_terms, tokens, g_wide))
    frozen = dot(tokens, base_weight, 1, 0)
    dx = dot(g_wide, base_weight, 1, 1)
    frozen, dx, dx_terms = lax.optimization_barrier((frozen, dx, dx_terms))
    frozen = lax.psum_scatter(frozen, ("mp", "sub"), scatter_dimension=1, tiled=True)
    dx_in = [shifted(t, (groups - s) % groups) for t, s in zip(dx_terms, steps)]

    x_here = jnp.concatenate(x_in, 0)
    x_here, back, dx = lax.optimization_barrier((x_here, back, dx))
    out_rank = lax.psum(fold(dot(x_here, down_rows, 1, 1)), ("mp", "sub")).astype(bf16)
    out_rank = spread(out_rank)
    out_term = (adapter_scale * dot(out_rank, up_rows, 1, 0)).astype(bf16)
    out_term = out_term.reshape(groups, slots, key_width)
    order = [lax.rem(me + 2 * groups - s - 1, groups) for s in range(groups)]
    out_term = jnp.stack(
        [lax.dynamic_index_in_dim(out_term, o, 0, keepdims=False) for o in order]
    )
    out_term, fullest = lax.optimization_barrier((out_term, fullest))
    out_term = swapped(out_term).reshape(groups * slots, key_width)
    fullest = lax.pmax(fullest, ("groups", "dp"))
    lora_out = dot(pick, out_term, 0, 0)

    down_grad = adapter_scale * dot(back, x_here, 0, 0)
    down_grad = jnp.transpose(down_grad.reshape(own, rank, width), (0, 2, 1))
    up_grad = (adapter_scale * dot(out_rank, g_here, 0, 0)).reshape(own, rank, key_width)
    down_grad, up_grad, dx, fullest = lax.optimization_barrier((down_grad, up_grad, dx, fullest))
    for term, step in zip(dx_in, steps):
        to = lax.rem(me + step, groups)
        hit = (holder[None, :] == to) & (place[None, :] == slot[:, None])
        dx = dx + dot(hit.astype(bf16), term, 0, 0)
    out = (frozen + lora_out).astype(bf16)
    return (out, dx.astype(bf16), down_grad, up_grad), fullest


def local(tokens, base_weight, down, up, cotangent, tenant):
    groups = lax.axis_size("dp")
    own = down.shape[0]
    most = own * (2 * tokens.shape[0] // (groups * own))
    usual = min(most, -(-(most * 13) // 256) * 16)
    ids = tenant[:, 0]
    holder = ids // own
    holds = holder[:, None] == jnp.arange(groups, dtype=jnp.int32)[None, :]
    counts = jnp.cumsum(holds.astype(jnp.int32), axis=0)
    place = jnp.sum(jnp.where(holds, counts - 1, 0), axis=1)
    args = (tokens, base_weight, down, up, cotangent, ids, holder, place, jnp.max(place))
    results, fullest = body(usual, *args)
    if usual == most:
        return results
    return lax.cond(fullest >= usual, lambda r: body(most, *args)[0], lambda r: r, results)


def solution(mesh):
    rows = P(("groups", "dp"), ("mp", "sub"))
    downs = P(("groups", "dp"), ("mp", "sub"), None)
    ups = P(("groups", "dp"), None, ("mp", "sub"))
    return jax.shard_map(
        local,
        mesh=mesh,
        in_specs=(rows, P(("mp", "sub"), None), downs, ups, rows, P(("groups", "dp"), None)),
        out_specs=(rows, rows, downs, ups),
        check_vma=False,
    )
```

```python
import functools

import jax
import jax.numpy as jnp
from jax import lax
from jax.sharding import PartitionSpec as P

adapter_scale = 0.5
f32 = jnp.float32
bf16 = jnp.bfloat16


def dot(a, b, ca, cb):
    return lax.dot_general(a, b, (((ca,), (cb,)), ((), ())), preferred_element_type=f32)


def body(slots, tokens, base_weight, down, up, cotangent, ids, holder, place):
    groups = lax.axis_size("dp")
    own, width, rank = down.shape
    rows = tokens.shape[0]
    key_width = cotangent.shape[1]
    me = lax.axis_index("dp")
    down_rows = jnp.transpose(down, (0, 2, 1)).reshape(own * rank, width)
    up_rows = up.reshape(own * rank, key_width)
    code_rows = -(-(own + 1) // 16) * 16
    g_wide = lax.all_gather(cotangent, ("mp", "sub"), axis=1, tiled=True)

    def shifted(array, step):
        if step == 0:
            return array
        return lax.ppermute(array, "dp", [(i, (i + step) % groups) for i in range(groups)])

    def swapped(array):
        return lax.all_to_all(array, "dp", split_axis=0, concat_axis=0, tiled=True)

    seat = holder * slots + place
    seats = jnp.arange(groups * slots, dtype=jnp.int32)
    pick = ((seat[None, :] == seats[:, None]) & (place < slots)[None, :]).astype(bf16)
    local_id = jnp.arange(code_rows, dtype=jnp.int32)
    code = (lax.rem(ids, own)[:, None] == local_id[None, :]).astype(bf16)
    code = dot(code, pick, 0, 1).astype(bf16).reshape(code_rows, groups, slots)
    full = (jnp.max(place) >= slots).astype(bf16)
    code = jnp.where(local_id[:, None, None] == own, full, code)
    code = jnp.pad(jnp.transpose(code, (1, 0, 2)), ((0, 0), (0, 0), (0, key_width - slots)))
    packed = dot(pick, cotangent, 1, 0).astype(bf16).reshape(groups, slots, key_width)
    packed = jnp.concatenate([packed, code], 1)
    packed, tokens = lax.optimization_barrier((packed, tokens))
    got = swapped(packed)

    slot = jnp.arange(slots, dtype=jnp.int32)
    steps = list(range(1, groups)) + [0]
    x_out = []
    for step in steps:
        to = lax.rem(me + step, groups)
        hit = (holder[None, :] == to) & (place[None, :] == slot[:, None])
        x_out.append(dot(hit.astype(bf16), tokens, 1, 0).astype(bf16))
    x_first = shifted(x_out[0], steps[0])
    x_out, got, tokens = lax.optimization_barrier((x_out, got, tokens))
    x_in = [x_first] + [shifted(x, step) for x, step in zip(x_out[1:], steps[1:])]
    sources = [lax.rem(me + groups - step, groups) for step in steps]

    got = [lax.dynamic_index_in_dim(got, source, 0, keepdims=False) for source in sources]
    g_here = jnp.concatenate([one[:slots] for one in got], 0)
    codes = jnp.concatenate([one[slots:, :slots] for one in got], 1)
    full = jnp.full((8, 128), jnp.max(codes[own]).astype(f32))
    copies = lax.axis_size("groups")
    fulls = [
        lax.ppermute(full, "groups", [(i, (i + k) % copies) for i in range(copies)])
        for k in range(1, copies)
    ]
    owner = jnp.arange(own * rank, dtype=jnp.int32) // rank
    mask = dot(codes, (local_id[:, None] == owner[None, :]).astype(bf16), 0, 0) > 0.5

    def fold(wide):
        return jnp.where(mask, wide, 0.0).reshape(-1, own, rank).sum(1)

    def spread(narrow):
        return jnp.where(mask, jnp.tile(narrow, (1, own)), jnp.zeros((), bf16))

    back = lax.psum(fold(dot(g_here, up_rows, 1, 1)), ("mp", "sub")).astype(bf16)
    back = spread(back)
    dx_terms = []
    for k, step in enumerate(steps):
        part = back[k * slots : (k + 1) * slots]
        dx_terms.append((adapter_scale * dot(part, down_rows, 1, 0)).astype(bf16))
    dx_terms, tokens, g_wide = lax.optimization_barrier((dx_terms, tokens, g_wide))
    frozen = dot(tokens, base_weight, 1, 0)
    dx = dot(g_wide, base_weight, 1, 1)
    frozen, dx, dx_terms = lax.optimization_barrier((frozen, dx, dx_terms))
    frozen = lax.psum_scatter(frozen, ("mp", "sub"), scatter_dimension=1, tiled=True)
    dx_in = [shifted(t, (groups - s) % groups) for t, s in zip(dx_terms, steps)]

    x_here = jnp.concatenate(x_in, 0)
    x_here, back, dx = lax.optimization_barrier((x_here, back, dx))
    out_rank = lax.psum(fold(dot(x_here, down_rows, 1, 1)), ("mp", "sub")).astype(bf16)
    out_rank = spread(out_rank)
    out_term = (adapter_scale * dot(out_rank, up_rows, 1, 0)).astype(bf16)
    out_term = out_term.reshape(groups, slots, key_width)
    order = [lax.rem(me + 2 * groups - s - 1, groups) for s in range(groups)]
    out_term = jnp.stack(
        [lax.dynamic_index_in_dim(out_term, o, 0, keepdims=False) for o in order]
    )
    out_term = swapped(out_term).reshape(groups * slots, key_width)
    lora_out = dot(pick, out_term, 0, 0)

    down_grad = adapter_scale * dot(back, x_here, 0, 0)
    down_grad = jnp.transpose(down_grad.reshape(own, rank, width), (0, 2, 1))
    up_grad = (adapter_scale * dot(out_rank, g_here, 0, 0)).reshape(own, rank, key_width)
    down_grad, up_grad, dx = lax.optimization_barrier((down_grad, up_grad, dx))
    for term, step in zip(dx_in, steps):
        to = lax.rem(me + step, groups)
        hit = (holder[None, :] == to) & (place[None, :] == slot[:, None])
        dx = dx + dot(hit.astype(bf16), term, 0, 0)
    out = (frozen + lora_out).astype(bf16)
    return (out, dx.astype(bf16), down_grad, up_grad), functools.reduce(jnp.maximum, fulls, full)[0, 0] > 0.5


def local(tokens, base_weight, down, up, cotangent, tenant):
    groups = lax.axis_size("dp")
    own = down.shape[0]
    most = own * (2 * tokens.shape[0] // (groups * own))
    usual = min(most, -(-(most * 13) // 256) * 16)
    ids = tenant[:, 0]
    holder = ids // own
    holds = holder[:, None] == jnp.arange(groups, dtype=jnp.int32)[None, :]
    counts = jnp.cumsum(holds.astype(jnp.int32), axis=0)
    place = jnp.sum(jnp.where(holds, counts - 1, 0), axis=1)
    args = (tokens, base_weight, down, up, cotangent, ids, holder, place)
    results, any_full = body(usual, *args)
    if usual == most:
        return results
    return lax.cond(any_full, lambda r: body(most, *args)[0], lambda r: r, results)


def solution(mesh):
    rows = P(("groups", "dp"), ("mp", "sub"))
    downs = P(("groups", "dp"), ("mp", "sub"), None)
    ups = P(("groups", "dp"), None, ("mp", "sub"))
    return jax.shard_map(
        local,
        mesh=mesh,
        in_specs=(rows, P(("mp", "sub"), None), downs, ups, rows, P(("groups", "dp"), None)),
        out_specs=(rows, rows, downs, ups),
        check_vma=False,
    )
```

```python
import jax
import jax.numpy as jnp
from jax import lax
from jax.sharding import PartitionSpec as P

adapter_scale = 0.5
f32 = jnp.float32
bf16 = jnp.bfloat16


def dot(a, b, ca, cb):
    return lax.dot_general(a, b, (((ca,), (cb,)), ((), ())), preferred_element_type=f32)


def body(slots, tokens, base_weight, down, up, cotangent, ids, holder, place):
    groups = lax.axis_size("dp")
    own, width, rank = down.shape
    rows = tokens.shape[0]
    key_width = cotangent.shape[1]
    me = lax.axis_index("dp")
    down_rows = jnp.transpose(down, (0, 2, 1)).reshape(own * rank, width)
    up_rows = up.reshape(own * rank, key_width)
    code_rows = -(-(own + 1) // 16) * 16
    g_wide = lax.all_gather(cotangent, ("mp", "sub"), axis=1, tiled=True)

    def shifted(array, step):
        if step == 0:
            return array
        return lax.ppermute(array, "dp", [(i, (i + step) % groups) for i in range(groups)])

    def swapped(array):
        return lax.all_to_all(array, "dp", split_axis=0, concat_axis=0, tiled=True)

    seat = holder * slots + place
    seats = jnp.arange(groups * slots, dtype=jnp.int32)
    pick = ((seat[None, :] == seats[:, None]) & (place < slots)[None, :]).astype(bf16)
    local_id = jnp.arange(code_rows, dtype=jnp.int32)
    code = (lax.rem(ids, own)[:, None] == local_id[None, :]).astype(bf16)
    code = dot(code, pick, 0, 1).astype(bf16).reshape(code_rows, groups, slots)
    full = (jnp.max(place) >= slots).astype(bf16)
    code = jnp.where(local_id[:, None, None] == own, full, code)
    code = jnp.pad(jnp.transpose(code, (1, 0, 2)), ((0, 0), (0, 0), (0, key_width - slots)))
    packed = dot(pick, cotangent, 1, 0).astype(bf16).reshape(groups, slots, key_width)
    packed = jnp.concatenate([packed, code], 1)
    packed, tokens = lax.optimization_barrier((packed, tokens))
    got = swapped(packed)

    slot = jnp.arange(slots, dtype=jnp.int32)
    steps = list(range(1, groups)) + [0]
    x_out = []
    for step in steps:
        to = lax.rem(me + step, groups)
        hit = (holder[None, :] == to) & (place[None, :] == slot[:, None])
        x_out.append(dot(hit.astype(bf16), tokens, 1, 0).astype(bf16))
    x_out, got, tokens = lax.optimization_barrier((x_out, got, tokens))
    x_in = [shifted(x, step) for x, step in zip(x_out, steps)]
    sources = [lax.rem(me + groups - step, groups) for step in steps]

    got = [lax.dynamic_index_in_dim(got, source, 0, keepdims=False) for source in sources]
    g_here = jnp.concatenate([one[:slots] for one in got], 0)
    codes = jnp.concatenate([one[slots:, :slots] for one in got], 1)
    full = jnp.full((8, 128), jnp.max(codes[own]).astype(f32))
    fulls = lax.all_gather(full, "groups", axis=0, tiled=True)
    owner = jnp.arange(own * rank, dtype=jnp.int32) // rank
    mask = dot(codes, (local_id[:, None] == owner[None, :]).astype(bf16), 0, 0) > 0.5

    def fold(wide):
        return jnp.where(mask, wide, 0.0).reshape(-1, own, rank).sum(1)

    def spread(narrow):
        return jnp.where(mask, jnp.tile(narrow, (1, own)), jnp.zeros((), bf16))

    back = lax.psum(fold(dot(g_here, up_rows, 1, 1)), ("mp", "sub")).astype(bf16)
    back = spread(back)
    dx_terms = []
    for k, step in enumerate(steps):
        part = back[k * slots : (k + 1) * slots]
        dx_terms.append((adapter_scale * dot(part, down_rows, 1, 0)).astype(bf16))
    dx_terms, tokens, g_wide = lax.optimization_barrier((dx_terms, tokens, g_wide))
    frozen = dot(tokens, base_weight, 1, 0)
    dx = dot(g_wide, base_weight, 1, 1)
    frozen, dx, dx_terms = lax.optimization_barrier((frozen, dx, dx_terms))
    frozen = lax.psum_scatter(frozen, ("mp", "sub"), scatter_dimension=1, tiled=True)
    dx_in = [shifted(t, (groups - s) % groups) for t, s in zip(dx_terms, steps)]

    x_here = jnp.concatenate(x_in, 0)
    x_here, back, dx = lax.optimization_barrier((x_here, back, dx))
    out_rank = lax.psum(fold(dot(x_here, down_rows, 1, 1)), ("mp", "sub")).astype(bf16)
    out_rank = spread(out_rank)
    out_term = (adapter_scale * dot(out_rank, up_rows, 1, 0)).astype(bf16)
    out_term = out_term.reshape(groups, slots, key_width)
    order = [lax.rem(me + 2 * groups - s - 1, groups) for s in range(groups)]
    out_term = jnp.stack(
        [lax.dynamic_index_in_dim(out_term, o, 0, keepdims=False) for o in order]
    )
    out_term = swapped(out_term).reshape(groups * slots, key_width)
    lora_out = dot(pick, out_term, 0, 0)

    down_grad = adapter_scale * dot(back, x_here, 0, 0)
    down_grad = jnp.transpose(down_grad.reshape(own, rank, width), (0, 2, 1))
    up_grad = (adapter_scale * dot(out_rank, g_here, 0, 0)).reshape(own, rank, key_width)
    down_grad, up_grad, dx = lax.optimization_barrier((down_grad, up_grad, dx))
    for term, step in zip(dx_in, steps):
        to = lax.rem(me + step, groups)
        hit = (holder[None, :] == to) & (place[None, :] == slot[:, None])
        dx = dx + dot(hit.astype(bf16), term, 0, 0)
    out = (frozen + lora_out).astype(bf16)
    return (out, dx.astype(bf16), down_grad, up_grad), jnp.max(fulls) > 0.5


def local(tokens, base_weight, down, up, cotangent, tenant):
    groups = lax.axis_size("dp")
    own = down.shape[0]
    most = own * (2 * tokens.shape[0] // (groups * own))
    usual = min(most, -(-(most * 13) // 256) * 16)
    ids = tenant[:, 0]
    holder = ids // own
    holds = holder[:, None] == jnp.arange(groups, dtype=jnp.int32)[None, :]
    counts = jnp.cumsum(holds.astype(jnp.int32), axis=0)
    place = jnp.sum(jnp.where(holds, counts - 1, 0), axis=1)
    args = (tokens, base_weight, down, up, cotangent, ids, holder, place)
    results, any_full = body(usual, *args)
    if usual == most:
        return results
    return lax.cond(any_full, lambda r: body(most, *args)[0], lambda r: r, results)


def solution(mesh):
    rows = P(("groups", "dp"), ("mp", "sub"))
    downs = P(("groups", "dp"), ("mp", "sub"), None)
    ups = P(("groups", "dp"), None, ("mp", "sub"))
    return jax.shard_map(
        local,
        mesh=mesh,
        in_specs=(rows, P(("mp", "sub"), None), downs, ups, rows, P(("groups", "dp"), None)),
        out_specs=(rows, rows, downs, ups),
        check_vma=False,
    )
```
